32 devices in a mesh: patch: 8 (over z, y), mp: 4 (over x, core).
Axes of the slice: x: 2, y: 2, z: 4, core: 2. Of those that a mesh axis runs over, the one named last changes fastest.
Arguments:
- grid_latent: bfloat16 [8192, 512], P('patch'), may hold values from -6 to 6
- mesh_latent: bfloat16 [1024, 512], P('patch', 'mp'), may hold values from -6 to 6
- edge_weight: bfloat16 [96, 128, 128], P('patch'), may hold values from -0.15625 to 0.15625
- block_source: int32 [96], P('patch'), may hold values from 0 to 63, as said below
- block_live: int32 [96], P('patch'), may hold values from 0 to 1
- mlp_first: bfloat16 [512, 512], replicated, may hold values from -0.25 to 0.25
- mlp_second: bfloat16 [512, 512], P(None, 'mp'), may hold values from -0.25 to 0.25
- mesh_cotangent: bfloat16 [1024, 512], P('patch', 'mp'), may hold values from -6 to 6
Outputs:
- mesh_out: bfloat16 [1024, 512], P('patch', 'mp')
- grad_first: float32 [512, 512], P(None, 'mp')
- grad_second: float32 [512, 512], P(None, 'mp')
The draws below stay inside these ranges and needn't reach their ends.
Inputs may be any that keep to these rules, and one draw needn't show every extreme that they name: `block_source`: grid patch g lies on the device of index g // 8 along patch, and slot b on the device of index b // 12. On every device at most 2 slots take their source from one device, and some device supplies exactly 2 slots to some device.
All inputs are finite; a program needn't handle non-finite values.
Results may differ from the reference program's by a relative error of at most 0.0058.
Values may be sent and summed in bfloat16 or wider, within the bound.
No kernel may reach another device: no remote copies, remote signals or barrier semaphores. Data moves between devices by JAX's collectives and lax.ppermute only.
A program may use at most 64 MiB of HBM per device.

```python
import math
import jax
import jax.numpy as jnp

D = 512
HID = 512
PATCH = 128
GPD = 8
BPM = 12
EBD = 12
NB = 96
NGP = 64
NG = 8192
NMP = 8
NM = 1024
N_PATCH = 8


def linked_blocks(key):
    slot_order = jnp.arange(EBD, dtype=jnp.int32)
    far_offset = N_PATCH // 2

    def receiver_lists(receiver, one_key):
        first_key, second_key, third_key = jax.random.split(one_key, 3)
        offsets = jax.random.permutation(first_key, N_PATCH).astype(jnp.int32)
        far_place = jnp.argmax((offsets == far_offset).astype(jnp.int32)).astype(jnp.int32)
        rolled = jnp.roll(offsets, -far_place)
        offsets = jnp.where(receiver == 0, rolled, offsets)
        chosen = offsets[jnp.mod(slot_order, N_PATCH)]
        source_device = jnp.mod(receiver + chosen, N_PATCH).astype(jnp.int32)
        patch_pick = jax.random.randint(second_key, (EBD,), 0, GPD).astype(jnp.int32)
        live = (jax.random.randint(third_key, (EBD,), 0, 3) > 0).astype(jnp.int32)
        live = jnp.where((receiver == 0) & (slot_order == 0), 1, live).astype(jnp.int32)
        return ((source_device * GPD + patch_pick).astype(jnp.int32), live)
    receivers = jnp.arange(N_PATCH, dtype=jnp.int32)
    keys = jax.random.split(jax.random.fold_in(key, 11), N_PATCH)
    global_id, flags = jax.vmap(receiver_lists)(receivers, keys)
    return (global_id.reshape(-1).astype(jnp.int32), flags.reshape(-1).astype(jnp.int32))


def draw_block_source(key, part):
    return linked_blocks(key)[0]


def draw_block_live(key, part):
    return linked_blocks(key)[1]


def levels(key, dims, cuts, low, top_value):
    loudness, own = 1.0, jax.random.fold_in(key, 6)
    for position, shards_of in cuts:
        draws = jnp.exp(jax.random.uniform(jax.random.fold_in(own, position), (shards_of,), jnp.float32, low / len(cuts), top_value / len(cuts)))
        loudness = loudness * jnp.repeat(draws, dims[position] // shards_of).reshape([-1 if axis == position else 1 for axis in range(len(dims))])
    return loudness


def bell_draw(own_key, extent, spread, bound, shards=(), kind=jnp.bfloat16):
    values = spread * jax.random.normal(own_key, extent, jnp.float32)
    if shards:
        values = values * levels(own_key, extent, shards, -0.22, 0.18)
    return jnp.clip(values, -bound, bound).astype(kind)


def setup_inputs(seed: int = 0) -> dict:
    key_of = jax.random.split(jax.random.key(seed), 9)
    return {
        "grid_latent": bell_draw(key_of[0], (NG, D), 1.0, 6.0, ((0, 8),)),
        "mesh_latent": bell_draw(key_of[1], (NM, D), 1.0, 6.0, ((0, 8), (1, 4))),
        "edge_weight": bell_draw(key_of[2], (NB, PATCH, PATCH), (PATCH * BPM) ** -0.5, 0.15625, ((0, 8),)),
        "block_source": draw_block_source(jax.random.fold_in(key_of[8], 71), 0),
        "block_live": draw_block_live(jax.random.fold_in(key_of[8], 71), 0),
        "mlp_first": bell_draw(key_of[5], (D, HID), D ** -0.5, 0.25),
        "mlp_second": bell_draw(key_of[6], (HID, D), HID ** -0.5, 0.25, ((1, 4),)),
        "mesh_cotangent": bell_draw(key_of[7], (NM, D), 1.0, 6.0, ((0, 8), (1, 4))),
    }


def silu_slope(values):
    sigmoid = jax.nn.sigmoid(values)
    return sigmoid * (1.0 + values * (1.0 - sigmoid))

def reference(grid_latent, mesh_latent, edge_weight, block_source, block_live, mlp_first, mlp_second, mesh_cotangent):
    pre_act = jnp.dot(grid_latent, mlp_first, preferred_element_type=jnp.float32)
    hidden = jax.nn.silu(pre_act).astype(jnp.bfloat16)
    message = jnp.dot(hidden, mlp_second, preferred_element_type=jnp.float32).astype(jnp.bfloat16)
    patches = message.reshape(NGP, PATCH, D)
    live_flag = block_live.astype(jnp.float32)[:, None, None]
    weights = edge_weight.astype(jnp.float32)
    sources = jnp.take(patches, block_source.astype(jnp.int32), axis=0).astype(jnp.float32)
    products = jnp.einsum('bpq,bqc->bpc', weights, sources) * live_flag
    summed = products.reshape(NMP, BPM, PATCH, D).sum(axis=1).reshape(NM, D)
    mesh_out = (mesh_latent.astype(jnp.float32) + summed).astype(jnp.bfloat16)
    cotangent = jnp.repeat(mesh_cotangent.reshape(NMP, PATCH, D), BPM, axis=0).astype(jnp.float32)
    adjoint = (jnp.einsum('bqp,bqc->bpc', weights, cotangent) * live_flag).astype(jnp.bfloat16)
    grad_message = jnp.zeros((NGP, PATCH, D), jnp.float32).at[block_source.astype(jnp.int32)].add(adjoint.astype(jnp.float32))
    grad_message = grad_message.reshape(NG, D).astype(jnp.bfloat16)
    scaling = 1.0 / math.sqrt(NG)
    grad_second = jnp.dot(hidden.T, grad_message, preferred_element_type=jnp.float32) * scaling
    grad_hidden = jnp.dot(grad_message, mlp_second.T, preferred_element_type=jnp.float32)
    grad_pre = (grad_hidden * silu_slope(pre_act)).astype(jnp.bfloat16)
    grad_first = jnp.dot(grid_latent.T, grad_pre, preferred_element_type=jnp.float32) * scaling
    return (mesh_out, grad_first, grad_second)
```

```python
import functools
import math

import jax
import jax.numpy as jnp
from jax import lax
from jax.experimental import pallas as pl
from jax.experimental.pallas import tpu as pltpu
from jax.sharding import PartitionSpec as P

BF16 = jnp.bfloat16
F32 = jnp.float32
INDEX_ROWS = 16
UNROLL = 8
VMEM_BYTES = 40 * 1024 * 1024


def dot(left, right):
    return jnp.dot(left, right, preferred_element_type=F32)


def whole(space=pltpu.VMEM):
    return pl.BlockSpec(memory_space=space)


def params():
    return pltpu.CompilerParams(vmem_limit_bytes=VMEM_BYTES)


def swap(value, axis, offset):
    size = lax.axis_size(axis)
    return lax.ppermute(value, axis, [(i, i ^ offset) for i in range(size)])


def each_device(count, body):
    group = min(count, UNROLL)
    if count == group:
        for step in range(count):
            body(step)
        return

    @pl.loop(0, count // group)
    def _(outer):
        for step in range(group):
            body(outer * group + step)


def pack_kernel(
    patches, cap, source, live, weight, cotangent, second, payload, kept, sent
):
    column = lax.axis_index("mp")
    slots, rows, width = weight.shape
    half = rows // 2
    devices = payload.shape[0]
    first_row = pl.multiple_of((column % 2) * half, half)
    turned = cotangent[...].T
    blank = jnp.zeros((cap * half, width), BF16)
    blank_index = jnp.zeros((INDEX_ROWS, width), BF16)

    def fill(device):
        payload[device, : cap * half] = blank
        payload[device, cap * half : cap * half + turned.shape[0]] = turned
        payload[device, cap * half + turned.shape[0] :] = blank_index

    each_device(devices, fill)
    row = lax.broadcasted_iota(jnp.int32, (INDEX_ROWS, width), 0)
    for slot in range(slots):
        device = source[slot] // patches
        place = source[slot] % patches
        rank = jnp.int32(0)
        for other in range(slot):
            same = (source[other] // patches == device) & (live[other] == 1)
            rank = rank + same.astype(jnp.int32)

        @pl.when(live[slot] == 1)
        def _():
            start = pl.multiple_of(rank * half, half)
            payload[device, pl.ds(start, half)] = weight[slot, pl.ds(first_row, half)]
            tail = pl.ds(cap * half + turned.shape[0], INDEX_ROWS)
            old = payload[device, tail].astype(F32)
            payload[device, tail] = jnp.where(row == rank, place.astype(F32), old).astype(BF16)

    term = lax.dot_general(
        second[...], cotangent[...], (((1,), (1,)), ((), ())), preferred_element_type=F32
    )
    block = term.shape[0] // 2
    upper = column >= lax.axis_size("mp") // 2
    kept[...] = jnp.where(upper, term[block:], term[:block])
    sent[...] = jnp.where(upper, term[:block], term[block:]).astype(BF16)


def local_kernel(latent, first, second, hidden, message, slope, scratch):
    column = lax.axis_index("mp")
    rows = latent.shape[0]
    own = slope.shape[0]
    tile = min(256, rows)
    for start in range(0, rows, tile):
        here = pl.ds(start, tile)
        pre = dot(latent[here], first[...])
        scratch[...] = pre
        value = (pre * jax.nn.sigmoid(pre)).astype(BF16)
        hidden[here] = value
        message[here] = dot(value, second[...]).astype(BF16)
        mine = scratch[:, pl.ds(pl.multiple_of(column * own, own), own)]
        gate = jax.nn.sigmoid(mine)
        slope[:, here] = (gate * (1.0 + mine * (1.0 - gate))).T


def adjoint_kernel(
    cap, scaling, places, received, other, message, hidden, forward, weights, second, total
):
    column = lax.axis_index("mp")
    devices, _, width = received.shape
    half = other.shape[1] // cap
    rows = 2 * half
    patches = message.shape[0] // rows
    mine = pl.ds(pl.multiple_of((column % 2) * half, half), half)
    theirs = pl.ds(pl.multiple_of((1 - column % 2) * half, half), half)
    total[...] = jnp.zeros_like(total)

    def one(device):
        turned = received[device, cap * half : cap * half + width]
        summed = None
        for rank in range(cap):
            slot = device * cap + rank
            place = places[slot]
            weights[slot, mine] = received[device, rank * half : (rank + 1) * half]
            weights[slot, theirs] = other[device, rank * half : (rank + 1) * half]
            block = weights[slot]
            start = pl.multiple_of(place * rows, rows)
            product = dot(block, message[pl.ds(start, rows)])
            summed = product if summed is None else summed + product
            total[place] += dot(turned, block).astype(BF16).astype(F32)
        forward[device] = summed.astype(BF16)

    each_device(devices, one)
    turned_message = jnp.concatenate(
        [total[place].astype(BF16) for place in range(patches)], axis=1
    )
    second[...] = (dot(turned_message, hidden[...]) * scaling).T.astype(BF16)


def first_kernel(cap, scaling, places, weights, carried, slope, latent, first, total):
    own = lax.axis_index("patch")
    devices = carried.shape[0]
    rows = weights.shape[1]
    patches = latent.shape[0] // rows
    total[...] = jnp.zeros_like(total)

    def one(offset):
        turned = carried[offset]
        device = jnp.bitwise_xor(own, offset)
        for rank in range(cap):
            slot = device * cap + rank
            total[places[slot]] += dot(turned, weights[slot])

    each_device(devices, one)
    grad_pre = jnp.concatenate(
        [
            (total[place] * slope[:, place * rows : (place + 1) * rows]).astype(BF16)
            for place in range(patches)
        ],
        axis=1,
    )
    first[...] = (dot(grad_pre, latent[...]) * scaling).T.astype(BF16)


def per_device(
    grid_latent,
    mesh_latent,
    edge_weight,
    block_source,
    block_live,
    mlp_first,
    mlp_second,
    mesh_cotangent,
):
    devices = lax.axis_size("patch")
    parts = lax.axis_size("mp")
    slots, rows, _ = edge_weight.shape
    grid_rows, depth = grid_latent.shape
    patches = grid_rows // rows
    hidden_width, width = mlp_second.shape
    hidden_local = hidden_width // parts
    cap = -(-slots // devices)
    half = rows // 2
    column = lax.axis_index("mp")
    scaling = 1.0 / math.sqrt(grid_rows * devices)
    payload_rows = cap * half + width + INDEX_ROWS

    payload, kept, sent = pl.pallas_call(
        functools.partial(pack_kernel, patches, cap),
        out_shape=(
            jax.ShapeDtypeStruct((devices, payload_rows, rows), BF16),
            jax.ShapeDtypeStruct((hidden_width // 2, rows), F32),
            jax.ShapeDtypeStruct((hidden_width // 2, rows), BF16),
        ),
        in_specs=[whole(pltpu.SMEM)] * 2 + [whole()] * 3,
        out_specs=(whole(),) * 3,
        compiler_params=params(),
        name="pack",
    )(block_source, block_live, edge_weight, mesh_cotangent, mlp_second)

    received = lax.all_to_all(payload, "patch", split_axis=0, concat_axis=0, tiled=True)

    carried = kept + swap(sent, "mp", parts // 2).astype(F32)
    offset = parts // 4
    while offset:
        size = carried.shape[0] // 2
        upper = (column // offset) % 2
        away = lax.dynamic_slice_in_dim(carried, (1 - upper) * size, size, 0)
        stay = lax.dynamic_slice_in_dim(carried, upper * size, size, 0)
        carried = stay + swap(away, "mp", offset)
        offset //= 2
    carried = carried.astype(BF16)[None]
    offset = 1
    while offset < devices:
        carried = jnp.concatenate([carried, swap(carried, "patch", offset)])
        offset *= 2

    hidden, message, slope = pl.pallas_call(
        local_kernel,
        out_shape=(
            jax.ShapeDtypeStruct((grid_rows, hidden_width), BF16),
            jax.ShapeDtypeStruct((grid_rows, width), BF16),
            jax.ShapeDtypeStruct((hidden_local, grid_rows), F32),
        ),
        in_specs=[whole()] * 3,
        out_specs=(whole(),) * 3,
        scratch_shapes=[pltpu.VMEM((min(256, grid_rows), hidden_width), F32)],
        compiler_params=params(),
        cost_estimate=pl.CostEstimate(
            flops=2 * grid_rows * hidden_width * (depth + width),
            bytes_accessed=4 * grid_rows * hidden_width,
            transcendentals=grid_rows * hidden_width,
        ),
        name="local",
    )(grid_latent, mlp_first, mlp_second)

    other = swap(received[:, : cap * half], "mp", 1)
    index_row = cap * half + width
    places = received[:, index_row : index_row + cap, 0].astype(jnp.int32).reshape(-1)

    forward, weights, grad_second = pl.pallas_call(
        functools.partial(adjoint_kernel, cap, scaling),
        out_shape=(
            jax.ShapeDtypeStruct((devices, rows, width), BF16),
            jax.ShapeDtypeStruct((devices * cap, rows, rows), BF16),
            jax.ShapeDtypeStruct((hidden_width, width), BF16),
        ),
        in_specs=[whole(pltpu.SMEM)] + [whole()] * 4,
        out_specs=(whole(),) * 3,
        scratch_shapes=[pltpu.VMEM((patches, width, rows), F32)],
        compiler_params=params(),
        name="adjoint",
    )(places, received, other, message, hidden)

    arrived = lax.all_to_all(forward, "patch", split_axis=0, concat_axis=0, tiled=True)
    mesh_out = (mesh_latent.astype(F32) + jnp.sum(arrived.astype(F32), axis=0)).astype(BF16)

    grad_first = pl.pallas_call(
        functools.partial(first_kernel, cap, scaling),
        out_shape=jax.ShapeDtypeStruct((depth, hidden_local), BF16),
        in_specs=[whole(pltpu.SMEM)] + [whole()] * 4,
        out_specs=whole(),
        scratch_shapes=[pltpu.VMEM((patches, hidden_local, rows), F32)],
        compiler_params=params(),
        name="first",
    )(places, weights, carried, slope, grid_latent)

    both = jnp.stack([grad_first, grad_second])
    offset = 1
    while offset < devices:
        both = both.astype(BF16)
        both = both.astype(F32) + swap(both, "patch", offset).astype(F32)
        offset *= 2
    return (mesh_out, both[0], both[1])


def solution(mesh):
    placed = (
        P("patch", None),
        P("patch", "mp"),
        P("patch", None, None),
        P("patch"),
        P("patch"),
        P(),
        P(None, "mp"),
        P("patch", "mp"),
    )
    return jax.shard_map(
        per_device,
        mesh=mesh,
        in_specs=placed,
        out_specs=(P("patch", "mp"), P(None, "mp"), P(None, "mp")),
        check_vma=False,
    )
```

```python
import functools
import math

import jax
import jax.numpy as jnp
from jax import lax
from jax.experimental import pallas as pl
from jax.experimental.pallas import tpu as pltpu
from jax.sharding import PartitionSpec as P

BF16 = jnp.bfloat16
F32 = jnp.float32
INDEX_ROWS = 16
UNROLL = 8
VMEM_BYTES = 16 * 1024 * 1024
VMEM = pltpu.VMEM
SMEM = pltpu.SMEM
HBM = pltpu.HBM


def dot(left, right):
    return jnp.dot(left, right, preferred_element_type=F32)


def call(kernel, name, placed, outputs, scratch=(), cost=None):
    return pl.pallas_call(
        kernel,
        out_shape=[VMEM(shape, dtype) for shape, dtype in outputs],
        in_specs=[pl.BlockSpec(memory_space=space) for space, _ in placed],
        out_specs=[pl.BlockSpec(memory_space=VMEM) for _ in outputs],
        scratch_shapes=list(scratch),
        compiler_params=pltpu.CompilerParams(vmem_limit_bytes=VMEM_BYTES),
        cost_estimate=cost,
        name=name,
    )(
        *[
            operand if space is SMEM else pltpu.with_memory_space_constraint(operand, space)
            for space, operand in placed
        ]
    )


def fetch(pairs, arrivals):
    copies = [
        pltpu.make_async_copy(source, target, arrivals.at[place])
        for place, (source, target) in enumerate(pairs)
    ]
    for copy in copies:
        copy.start()
    return copies


def after(value, *others):
    return lax.optimization_barrier((value, *others))[0]


def swap(value, axis, offset):
    size = lax.axis_size(axis)
    return lax.ppermute(value, axis, [(i, i ^ offset) for i in range(size)])


def each_device(count, body):
    group = min(count, UNROLL)
    if count == group:
        for step in range(count):
            body(step)
        return

    @pl.loop(0, count // group)
    def _(outer):
        for step in range(group):
            body(outer * group + step)


def term_kernel(
    cotangent_hbm, second_hbm, kept, sent, turned, cotangent, second, arrivals
):
    for copy in fetch([(cotangent_hbm, cotangent), (second_hbm, second)], arrivals):
        copy.wait()
    turned[...] = cotangent[...].T
    column = lax.axis_index("mp")
    term = lax.dot_general(
        second[...], cotangent[...], (((1,), (1,)), ((), ())), preferred_element_type=F32
    )
    block = term.shape[0] // 2
    upper = column >= lax.axis_size("mp") // 2
    kept[...] = jnp.where(upper, term[block:], term[:block])
    sent[...] = jnp.where(upper, term[:block], term[block:]).astype(BF16)


def pack_kernel(
    patches, cap, source_hbm, live_hbm, weight_hbm, payload, source, live, weight, arrivals
):
    column = lax.axis_index("mp")
    slots, half, width = weight.shape
    devices = payload.shape[0]
    first_row = pl.multiple_of((column % 2) * half, half)
    copies = fetch(
        [
            (source_hbm, source),
            (live_hbm, live),
            (weight_hbm.at[:, pl.ds(first_row, half)], weight),
        ],
        arrivals,
    )
    blank = jnp.zeros(payload.shape[1:], BF16)
    tail = cap * half
    row = lax.broadcasted_iota(jnp.int32, (INDEX_ROWS, width), 0)

    def clear(device):
        payload[device] = blank

    each_device(devices, clear)
    for copy in copies:
        copy.wait()
    for slot in range(slots):
        device = source[slot] // patches
        place = source[slot] % patches
        rank = jnp.int32(0)
        for other in range(slot):
            same = (source[other] // patches == device) & (live[other] == 1)
            rank = rank + same.astype(jnp.int32)

        @pl.when(live[slot] == 1)
        def _():
            payload[device, pl.ds(pl.multiple_of(rank * half, half), half)] = weight[slot]
            old = payload[device, tail:].astype(F32)
            payload[device, tail:] = jnp.where(row == rank, place.astype(F32), old).astype(BF16)


def local_kernel(latent, first, second, hidden, message, slope, scratch):
    column = lax.axis_index("mp")
    rows = latent.shape[0]
    own = slope.shape[0]
    tile = min(256, rows)
    for start in range(0, rows, tile):
        here = pl.ds(start, tile)
        pre = dot(latent[here], first[...])
        scratch[...] = pre
        value = (pre * jax.nn.sigmoid(pre)).astype(BF16)
        hidden[here] = value
        message[here] = dot(value, second[...]).astype(BF16)
        mine = scratch[:, pl.ds(pl.multiple_of(column * own, own), own)]
        gate = jax.nn.sigmoid(mine)
        slope[:, here] = (gate * (1.0 + mine * (1.0 - gate))).T


def carried_device(step, held_near, offsets):
    device = lax.axis_index("patch")
    if not held_near:
        device = device ^ offsets[-1]
    for place, offset in enumerate(offsets[:-1]):
        device = device ^ (((step >> place) & 1) * offset)
    return device


def adjoint_kernel(
    cap,
    gather_order,
    sum_order,
    scaling,
    places,
    received,
    other,
    near,
    far,
    message,
    hidden,
    sent,
    kept,
    weights,
    total,
):
    column = lax.axis_index("mp")
    own = lax.axis_index("patch")
    devices, _, rows = received.shape
    half = other.shape[1] // cap
    width = message.shape[1]
    patches = message.shape[0] // rows
    mine = pl.ds(pl.multiple_of((column % 2) * half, half), half)
    theirs = pl.ds(pl.multiple_of((1 - column % 2) * half, half), half)
    total[...] = jnp.zeros_like(total)

    def one(step, held, is_near):
        device = carried_device(step, is_near, gather_order)
        turned = held[step, :width]
        summed = None
        for rank in range(cap):
            slot = device * cap + rank
            place = places[slot]
            weights[slot, mine] = received[device, rank * half : (rank + 1) * half]
            weights[slot, theirs] = other[device, rank * half : (rank + 1) * half]
            block = weights[slot]
            start = pl.multiple_of(place * rows, rows)
            product = dot(block, message[pl.ds(start, rows)])
            summed = product if summed is None else summed + product
            total[place] += dot(turned, block).astype(BF16).astype(F32)
        apart = device ^ own
        away = (apart // sum_order[0]) & 1
        block = jnp.int32(0)
        for offset in sum_order[1:]:
            block = 2 * block + ((apart // offset) & 1)

        @pl.when(away == 1)
        def _():
            start = pl.multiple_of(hidden.shape[1] + block * rows, rows)
            sent[pl.ds(start, rows)] = summed.astype(BF16)

        @pl.when(away == 0)
        def _():
            kept[pl.ds(pl.multiple_of(block * rows, rows), rows)] = summed

    each_device(devices // 2, lambda step: one(step, near, True))
    each_device(devices // 2, lambda step: one(step, far, False))
    turned_message = jnp.concatenate(
        [total[place].astype(BF16) for place in range(patches)], axis=1
    )
    second = dot(turned_message, hidden[...]) * scaling
    sent[: hidden.shape[1]] = second.T.astype(BF16)


def first_kernel(
    cap, gather_order, scaling, places, weights, near, far, slope, latent, first, total
):
    devices = 2 * near.shape[0]
    rows = weights.shape[1]
    width = near.shape[1] - slope.shape[0]
    patches = latent.shape[0] // rows
    total[...] = jnp.zeros_like(total)

    def one(step, held, is_near):
        device = carried_device(step, is_near, gather_order)
        turned = held[step, width:]
        for rank in range(cap):
            slot = device * cap + rank
            total[places[slot]] += dot(turned, weights[slot])

    each_device(devices // 2, lambda step: one(step, near, True))
    each_device(devices // 2, lambda step: one(step, far, False))
    grad_pre = jnp.concatenate(
        [
            (total[place] * slope[:, place * rows : (place + 1) * rows]).astype(BF16)
            for place in range(patches)
        ],
        axis=1,
    )
    first[...] = (dot(grad_pre, latent[...]) * scaling).T.astype(BF16)


def per_device(
    grid_latent,
    mesh_latent,
    edge_weight,
    block_source,
    block_live,
    mlp_first,
    mlp_second,
    mesh_cotangent,
):
    devices = lax.axis_size("patch")
    parts = lax.axis_size("mp")
    slots, rows, _ = edge_weight.shape
    grid_rows, depth = grid_latent.shape
    patches = grid_rows // rows
    hidden_width, width = mlp_second.shape
    hidden_local = hidden_width // parts
    cap = -(-slots // devices)
    half = rows // 2
    column = lax.axis_index("mp")
    scaling = 1.0 / math.sqrt(grid_rows * devices)
    payload_rows = cap * half + INDEX_ROWS

    slot_bytes = ((slots,), jnp.int32)
    kept, sent, turned = call(
        term_kernel,
        "term",
        [(HBM, mesh_cotangent), (HBM, mlp_second)],
        [
            ((hidden_width // 2, rows), F32),
            ((hidden_width // 2, rows), BF16),
            ((width, rows), BF16),
        ],
        scratch=[
            VMEM(mesh_cotangent.shape, BF16),
            VMEM(mlp_second.shape, BF16),
            pltpu.SemaphoreType.DMA((2,)),
        ],
    )
    (payload,) = call(
        functools.partial(pack_kernel, patches, cap),
        "pack",
        [(HBM, block_source), (HBM, block_live), (HBM, edge_weight)],
        [((devices, payload_rows, rows), BF16)],
        scratch=[
            SMEM(*slot_bytes),
            SMEM(*slot_bytes),
            VMEM((slots, half, rows), BF16),
            pltpu.SemaphoreType.DMA((3,)),
        ],
    )

    carried = after(kept, payload) + swap(sent, "mp", parts // 2).astype(F32)
    offset = parts // 4
    while offset:
        size = carried.shape[0] // 2
        upper = (column // offset) % 2
        away = lax.dynamic_slice_in_dim(carried, (1 - upper) * size, size, 0)
        stay = lax.dynamic_slice_in_dim(carried, upper * size, size, 0)
        carried = stay + swap(away, "mp", offset)
        offset //= 2
    carried = jnp.concatenate([turned, carried.astype(BF16)])[None]
    hidden, message, slope = call(
        local_kernel,
        "local",
        [(VMEM, grid_latent), (VMEM, mlp_first), (VMEM, mlp_second)],
        [
            ((grid_rows, hidden_width), BF16),
            ((grid_rows, width), BF16),
            ((hidden_local, grid_rows), F32),
        ],
        scratch=[VMEM((min(256, grid_rows), hidden_width), F32)],
    )

    steps = devices.bit_length() - 1
    up = [1 << place for place in range(steps)]
    down = up[::-1]
    gather_order, second_order, first_order = down[:1] + up[:-1], up, up[1:] + up[:1]
    near = carried
    for offset in gather_order:
        if offset != gather_order[0]:
            near = jnp.concatenate([near, far])
        far = swap(near, "patch", offset)
        if offset == gather_order[min(1, steps - 1)]:
            far = after(far, hidden)
        if offset == gather_order[0]:
            payload = after(payload, far)
            received = lax.all_to_all(payload, "patch", split_axis=0, concat_axis=0, tiled=True)
    other = swap(received[:, : cap * half], "mp", 1)
    index_row = cap * half
    places = received[:, index_row : index_row + cap, 0].astype(jnp.int32).reshape(-1)

    sent, kept, weights = call(
        functools.partial(adjoint_kernel, cap, gather_order, second_order, scaling),
        "adjoint",
        [
            (SMEM, places),
            (VMEM, received),
            (VMEM, other),
            (VMEM, near),
            (VMEM, far),
            (VMEM, message),
            (VMEM, hidden),
        ],
        [
            ((hidden_width + devices // 2 * rows, width), BF16),
            ((devices // 2 * rows, width), F32),
            ((devices * cap, rows, rows), BF16),
        ],
        scratch=[VMEM((patches, width, rows), F32)],
    )
    (grad_first,) = call(
        functools.partial(first_kernel, cap, gather_order, scaling),
        "first",
        [
            (SMEM, places),
            (VMEM, weights),
            (VMEM, near),
            (VMEM, far),
            (VMEM, slope),
            (VMEM, grid_latent),
        ],
        [((depth, hidden_local), BF16)],
        scratch=[VMEM((patches, hidden_local, rows), F32)],
    )

    first = grad_first
    for step in range(steps):
        if step:
            size = kept.shape[0] // 2
            sent = jnp.concatenate([second, kept[size:]]).astype(BF16)
            kept = kept[:size]
            first = first.astype(BF16)
        got = swap(sent, "patch", second_order[step]).astype(F32)
        second = sent[:hidden_width].astype(F32) + got[:hidden_width]
        kept = kept + got[hidden_width:]
        if step == steps - 1:
            mesh_out = (mesh_latent.astype(F32) + kept).astype(BF16)
        first = first.astype(F32) + swap(first, "patch", first_order[step]).astype(F32)
    return (mesh_out, first, second)


def solution(mesh):
    placed = (
        P("patch", None),
        P("patch", "mp"),
        P("patch", None, None),
        P("patch"),
        P("patch"),
        P(),
        P(None, "mp"),
        P("patch", "mp"),
    )
    return jax.shard_map(
        per_device,
        mesh=mesh,
        in_specs=placed,
        out_specs=(P("patch", "mp"), P(None, "mp"), P(None, "mp")),
        check_vma=False,
    )
```

```python
import functools
import math

import jax
import jax.numpy as jnp
from jax import lax
from jax.experimental import pallas as pl
from jax.experimental.pallas import tpu as pltpu
from jax.sharding import PartitionSpec as P

BF16 = jnp.bfloat16
F32 = jnp.float32
INDEX_ROWS = 16
UNROLL = 8
VMEM_BYTES = 16 * 1024 * 1024
VMEM = pltpu.VMEM
SMEM = pltpu.SMEM
HBM = pltpu.HBM


def dot(left, right):
    return jnp.dot(left, right, preferred_element_type=F32)


def call(kernel, name, placed, outputs, scratch=(), cost=None):
    return pl.pallas_call(
        kernel,
        out_shape=[space(shape, dtype) for space, shape, dtype in outputs],
        in_specs=[pl.BlockSpec(memory_space=space) for space, _ in placed],
        out_specs=[pl.BlockSpec(memory_space=space) for space, _, _ in outputs],
        scratch_shapes=list(scratch),
        compiler_params=pltpu.CompilerParams(vmem_limit_bytes=VMEM_BYTES),
        cost_estimate=cost,
        name=name,
    )(
        *[
            operand if space is SMEM else pltpu.with_memory_space_constraint(operand, space)
            for space, operand in placed
        ]
    )


def fetch(pairs, arrivals):
    copies = [
        pltpu.make_async_copy(source, target, arrivals.at[place])
        for place, (source, target) in enumerate(pairs)
    ]
    for copy in copies:
        copy.start()
    return copies


def after(value, *others):
    return lax.optimization_barrier((value, *others))[0]


def swap(value, axis, offset):
    size = lax.axis_size(axis)
    return lax.ppermute(value, axis, [(i, i ^ offset) for i in range(size)])


def spread(value, group):
    devices, parts = lax.axis_size("patch"), lax.axis_size("mp")
    pairs = [
        (device * parts + column, (device ^ (column + parts * group)) * parts + column)
        for device in range(devices)
        for column in range(parts)
    ]
    return lax.ppermute(value, ("patch", "mp"), pairs)


def swap_both(value, offset, column_offset):
    devices, parts = lax.axis_size("patch"), lax.axis_size("mp")
    pairs = [
        (device * parts + column, (device ^ offset) * parts + (column ^ column_offset))
        for device in range(devices)
        for column in range(parts)
    ]
    return lax.ppermute(value, ("patch", "mp"), pairs)


def each_device(count, body):
    group = min(count, UNROLL)
    if count == group:
        for step in range(count):
            body(step)
        return

    @pl.loop(0, count // group)
    def _(outer):
        for step in range(group):
            body(outer * group + step)


def term_kernel(
    cotangent_hbm, second_hbm, kept, sent, turned, cotangent, second, arrivals
):
    for copy in fetch([(cotangent_hbm, cotangent), (second_hbm, second)], arrivals):
        copy.wait()
    turned[...] = cotangent[...].T
    parts = lax.axis_size("mp")
    odd = lax.axis_index("mp") % 2 == 1
    term = lax.dot_general(
        second[...], cotangent[...], (((1,), (1,)), ((), ())), preferred_element_type=F32
    )
    size = term.shape[0] // parts
    for pair in range(parts // 2):
        even_block = term[2 * pair * size : (2 * pair + 1) * size]
        odd_block = term[(2 * pair + 1) * size : (2 * pair + 2) * size]
        kept[pair] = jnp.where(odd, odd_block, even_block)
        sent[pair] = jnp.where(odd, even_block, odd_block)


def pack_kernel(
    patches, cap, source_hbm, live_hbm, weight_hbm, payload, source, live, weight, arrivals
):
    own, column = lax.axis_index("patch"), lax.axis_index("mp")
    parts = lax.axis_size("mp")
    slots, rows, width = weight.shape
    copies = fetch([(source_hbm, source), (live_hbm, live), (weight_hbm, weight)], arrivals)
    tail = cap * rows
    row = lax.broadcasted_iota(jnp.int32, (INDEX_ROWS, width), 0)
    payload[...] = jnp.zeros_like(payload)
    for copy in copies:
        copy.wait()
    for slot in range(slots):
        device = source[slot] // patches
        place = source[slot] % patches
        rank = jnp.int32(0)
        for other in range(slot):
            same = (source[other] // patches == device) & (live[other] == 1)
            rank = rank + same.astype(jnp.int32)
        apart = device ^ own

        @pl.when((live[slot] == 1) & (apart % parts == column))
        def _():
            group = apart // parts
            payload[group, pl.ds(pl.multiple_of(rank * rows, rows), rows)] = weight[slot]
            old = payload[group, tail:].astype(F32)
            payload[group, tail:] = jnp.where(row == rank, place.astype(F32), old).astype(BF16)


def local_kernel(latent, first, second, hidden, message, slope, scratch):
    column = lax.axis_index("mp")
    rows = latent.shape[0]
    own = slope.shape[0]
    tile = min(256, rows)
    for start in range(0, rows, tile):
        here = pl.ds(start, tile)
        pre = dot(latent[here], first[...])
        scratch[...] = pre
        value = (pre * jax.nn.sigmoid(pre)).astype(BF16)
        hidden[here] = value
        message[here] = dot(value, second[...]).astype(BF16)
        mine = scratch[:, pl.ds(pl.multiple_of(column * own, own), own)]
        gate = jax.nn.sigmoid(mine)
        slope[:, here] = (gate * (1.0 + mine * (1.0 - gate))).T


def each_block(near, far, gather_order, body):
    own, column = lax.axis_index("patch"), lax.axis_index("mp")
    sides, groups = near.shape[:2]
    for turn in range(2 * sides):
        held = far if turn % 2 else near

        def one(group):
            apart = (column ^ turn) + 2 * sides * group
            position = jnp.int32(0)
            for place, offset in enumerate(gather_order):
                position = position + (((apart // offset) & 1) << place)
            number = turn * groups + group
            body(held.at[turn // 2, group], own ^ apart, position, number)

        each_device(groups, one)


def spot(apart, order):
    number = jnp.int32(0)
    for offset in order:
        number = 2 * number + ((apart // offset) & 1)
    return number


def halve(value, offset, sent, kept):
    half = value.shape[0] // 2
    upper = (lax.axis_index("patch") // offset) % 2 == 1
    kept[...] = jnp.where(upper, value[half:], value[:half])
    sent[:half] = jnp.where(upper, value[:half], value[half:]).astype(BF16)


def gradient_kernel(
    cap,
    gather_order,
    second_order,
    first_order,
    scaling,
    places,
    near,
    far,
    carried,
    message,
    hidden,
    slope_hbm,
    latent,
    sent_second,
    kept_second,
    forward,
    sent_first,
    kept_first,
    terms,
    forwards,
    total,
    slope,
    arrivals,
):
    copies = fetch([(slope_hbm, slope)], arrivals)
    own = lax.axis_index("patch")
    width = message.shape[1]
    rows = near.shape[3]
    patches = message.shape[0] // rows

    def one(held, device, position, number):
        turned = carried[position]
        summed = None
        for rank in range(cap):
            place = places[number * cap + rank]
            block = held[rank * rows : (rank + 1) * rows]
            start = pl.multiple_of(place * rows, rows)
            product = dot(block, message[pl.ds(start, rows)])
            summed = product if summed is None else summed + product
            terms[number * cap + rank] = dot(turned, block)
        forwards[spot(device ^ own, second_order)] = summed

    each_block(near, far, gather_order, one)
    total[...] = jnp.zeros_like(total)

    def add(slot):
        place = places[slot]
        term = terms[slot]
        total[place, :width] += term[:width].astype(BF16).astype(F32)
        total[place, width:] += term[width:]

    each_device(terms.shape[0], add)
    turned_message = jnp.concatenate(
        [total[place, :width].astype(BF16) for place in range(patches)], axis=1
    )
    second = dot(turned_message, hidden[...]) * scaling
    halve(second.T, second_order[0], sent_second, kept_second)
    for copy in copies:
        copy.wait()
    grad_pre = jnp.concatenate(
        [
            (total[place, width:] * slope[:, place * rows : (place + 1) * rows]).astype(BF16)
            for place in range(patches)
        ],
        axis=1,
    )
    first = dot(grad_pre, latent[...]) * scaling
    halve(first.T, first_order[0], sent_first, kept_first)
    devices = forwards.shape[0]
    split = kept_second.shape[0]
    for device in range(devices // 2):
        here = device * rows
        forward[here : here + rows] = forwards[device]
        sent_second[split + here : split + here + rows] = forwards[
            devices // 2 + device
        ].astype(BF16)


def finish_kernel(
    second_offset,
    first_offset,
    mesh_latent,
    forward,
    own_second,
    got_second,
    own_first,
    got_first,
    mesh_hbm,
    first_hbm,
    second_hbm,
    mesh,
    first,
    second,
    departures,
):
    mesh[...] = (mesh_latent[...].astype(F32) + forward[...]).astype(BF16)
    copies = []
    for place, offset, own, got, whole, target in (
        (0, second_offset, own_second, got_second, second, second_hbm),
        (1, first_offset, own_first, got_first, first, first_hbm),
    ):
        half = own.shape[0]
        upper = (lax.axis_index("patch") // offset) % 2
        whole[pl.ds(pl.multiple_of(upper * half, half), half)] = own[...].astype(F32)
        whole[pl.ds(pl.multiple_of((1 - upper) * half, half), half)] = got[...].astype(F32)
        copies.append(pltpu.make_async_copy(whole, target, departures.at[place]))
        copies[-1].start()
    copies.append(pltpu.make_async_copy(mesh, mesh_hbm, departures.at[2]))
    copies[-1].start()
    for copy in copies:
        copy.wait()


def per_device(
    grid_latent,
    mesh_latent,
    edge_weight,
    block_source,
    block_live,
    mlp_first,
    mlp_second,
    mesh_cotangent,
):
    devices = lax.axis_size("patch")
    parts = lax.axis_size("mp")
    slots, rows, _ = edge_weight.shape
    grid_rows, depth = grid_latent.shape
    patches = grid_rows // rows
    hidden_width, width = mlp_second.shape
    hidden_local = hidden_width // parts
    cap = -(-slots // devices)
    column = lax.axis_index("mp")
    scaling = 1.0 / math.sqrt(grid_rows * devices)
    payload_rows = cap * rows + INDEX_ROWS
    groups = devices // parts

    slot_bytes = ((slots,), jnp.int32)
    kept, sent, turned = call(
        term_kernel,
        "term",
        [(HBM, mesh_cotangent), (HBM, mlp_second)],
        [
            (VMEM, (parts // 2, hidden_local, rows), F32),
            (VMEM, (parts // 2, hidden_local, rows), F32),
            (VMEM, (width, rows), BF16),
        ],
        scratch=[
            VMEM(mesh_cotangent.shape, BF16),
            VMEM(mlp_second.shape, BF16),
            pltpu.SemaphoreType.DMA((2,)),
        ],
    )
    (payload,) = call(
        functools.partial(pack_kernel, patches, cap),
        "pack",
        [(HBM, block_source), (HBM, block_live), (HBM, edge_weight)],
        [(VMEM, (groups, payload_rows, rows), BF16)],
        scratch=[
            SMEM(*slot_bytes),
            SMEM(*slot_bytes),
            VMEM(edge_weight.shape, BF16),
            pltpu.SemaphoreType.DMA((3,)),
        ],
    )

    summed = after(kept, payload) + swap(sent, "mp", 1)
    offset = 2
    while summed.shape[0] > 2:
        pairs = summed.reshape(-1, 2, *summed.shape[1:])
        bit = (column // offset) % 2
        stay = lax.dynamic_index_in_dim(pairs, bit, 1, keepdims=False)
        away = lax.dynamic_index_in_dim(pairs, 1 - bit, 1, keepdims=False)
        summed = stay + swap(away, "mp", offset)
        offset *= 2
    bit = (column // offset) % 2
    stay = lax.dynamic_index_in_dim(summed, bit, 0, keepdims=False)
    away = lax.dynamic_index_in_dim(summed, 1 - bit, 0, keepdims=False).astype(BF16)
    steps = devices.bit_length() - 1
    up = [1 << place for place in range(steps)]
    down = up[::-1]
    gather_order, second_order, first_order = down[:1] + up[:-1], [*up[1::-1], *up[2:]], up
    across = gather_order[0]
    beside = swap(away, "mp", offset)
    facing = swap(jnp.concatenate([turned, stay.astype(BF16)]), "patch", across)
    corner = swap_both(away, across, offset)
    here = jnp.concatenate([turned, (stay + beside.astype(F32)).astype(BF16)])
    there = facing[width:].astype(F32) + corner.astype(F32)
    there = jnp.concatenate([facing[:width], there.astype(BF16)])
    carried = jnp.stack([here, there])

    latent = after(grid_latent, carried)
    hidden, message, slope = call(
        local_kernel,
        "local",
        [(VMEM, latent), (VMEM, mlp_first), (VMEM, mlp_second)],
        [
            (VMEM, (grid_rows, hidden_width), BF16),
            (VMEM, (grid_rows, width), BF16),
            (VMEM, (hidden_local, grid_rows), F32),
        ],
        scratch=[VMEM((min(256, grid_rows), hidden_width), F32)],
    )

    payload = after(payload, beside)
    spreads = [spread(payload[group], group) for group in range(groups)]
    for place in range(1, steps, 2):
        moves = gather_order[place : place + 2]
        offsets = [moves[0]] if len(moves) == 1 else [moves[0], moves[1], moves[0] ^ moves[1]]
        arriving = [swap(carried, "patch", offset) for offset in offsets]
        if place == 1:
            arriving[0] = after(arriving[0], hidden)
        carried = jnp.concatenate([carried, *arriving])

    blocks = after(jnp.stack(spreads), hidden)
    near = blocks[None]
    offset = parts // 2
    while offset > 1:
        near = jnp.concatenate([near, swap(near, "mp", offset)])
        offset //= 2
    far = swap(near, "mp", 1)
    index_row = cap * rows
    places = jnp.stack([near, far], axis=1)[..., index_row : index_row + cap, 0]
    places = places.astype(jnp.int32).reshape(-1)

    sent_second, kept_second, forward, sent_first, kept_first = call(
        functools.partial(
            gradient_kernel, cap, gather_order, second_order, first_order, scaling
        ),
        "gradients",
        [
            (SMEM, places),
            (VMEM, near),
            (VMEM, far),
            (VMEM, carried),
            (VMEM, message),
            (VMEM, hidden),
            (HBM, slope),
            (VMEM, latent),
        ],
        [
            (VMEM, (hidden_width // 2 + devices // 2 * rows, width), BF16),
            (VMEM, (hidden_width // 2, width), F32),
            (VMEM, (devices // 2 * rows, width), F32),
            (VMEM, (depth // 2, hidden_local), BF16),
            (VMEM, (depth // 2, hidden_local), F32),
        ],
        scratch=[
            VMEM((devices * cap, width + hidden_local, rows), F32),
            VMEM((devices, rows, width), F32),
            VMEM((patches, width + hidden_local, rows), F32),
            VMEM(slope.shape, F32),
            pltpu.SemaphoreType.DMA((1,)),
        ],
    )

    split = hidden_width // 2
    for step in range(steps):
        got_second = swap(sent_second, "patch", second_order[step]).astype(F32)
        got_first = swap(sent_first, "patch", first_order[step]).astype(F32)
        second = kept_second + got_second[:split]
        forward = forward + got_second[split:]
        sent_first = (kept_first + got_first).astype(BF16)
        if step < steps - 1:
            size = forward.shape[0] // 2
            sent_second = jnp.concatenate([second, forward[size:]]).astype(BF16)
            forward = forward[:size]
            kept_second = sent_second[:split].astype(F32)
            kept_first = sent_first.astype(F32)
    second = second.astype(BF16)
    mesh_out, first, second = call(
        functools.partial(finish_kernel, second_order[0], first_order[0]),
        "finish",
        [
            (VMEM, mesh_latent),
            (VMEM, forward),
            (VMEM, second),
            (VMEM, swap(second, "patch", second_order[0])),
            (VMEM, sent_first),
            (VMEM, swap(sent_first, "patch", first_order[0])),
        ],
        [
            (HBM, (rows, width), BF16),
            (HBM, (depth, hidden_local), F32),
            (HBM, (hidden_width, width), F32),
        ],
        scratch=[
            VMEM((rows, width), BF16),
            VMEM((depth, hidden_local), F32),
            VMEM((hidden_width, width), F32),
            pltpu.SemaphoreType.DMA((3,)),
        ],
    )
    return (mesh_out, first, second)


def solution(mesh):
    placed = (
        P("patch", None),
        P("patch", "mp"),
        P("patch", None, None),
        P("patch"),
        P("patch"),
        P(),
        P(None, "mp"),
        P("patch", "mp"),
    )
    return jax.shard_map(
        per_device,
        mesh=mesh,
        in_specs=placed,
        out_specs=(P("patch", "mp"), P(None, "mp"), P(None, "mp")),
        check_vma=False,
    )
```

```python
import functools
import math

import jax
import jax.numpy as jnp
from jax import lax
from jax.experimental import pallas as pl
from jax.experimental.pallas import tpu as pltpu
from jax.sharding import PartitionSpec as P

BF16 = jnp.bfloat16
F32 = jnp.float32
INDEX_ROWS = 16
UNROLL = 8
VMEM_BYTES = 16 * 1024 * 1024
VMEM = pltpu.VMEM
SMEM = pltpu.SMEM
HBM = pltpu.HBM


def dot(left, right):
    return jnp.dot(left, right, preferred_element_type=F32)


def call(kernel, name, placed, outputs, scratch=(), cost=None):
    return pl.pallas_call(
        kernel,
        out_shape=[space(shape, dtype) for space, shape, dtype in outputs],
        in_specs=[pl.BlockSpec(memory_space=space) for space, _ in placed],
        out_specs=[pl.BlockSpec(memory_space=space) for space, _, _ in outputs],
        scratch_shapes=list(scratch),
        compiler_params=pltpu.CompilerParams(vmem_limit_bytes=VMEM_BYTES),
        cost_estimate=cost,
        name=name,
    )(
        *[
            operand if space is SMEM else pltpu.with_memory_space_constraint(operand, space)
            for space, operand in placed
        ]
    )


def fetch(pairs, arrivals):
    copies = [
        pltpu.make_async_copy(source, target, arrivals.at[place])
        for place, (source, target) in enumerate(pairs)
    ]
    for copy in copies:
        copy.start()
    return copies


def after(value, *others):
    return lax.optimization_barrier((value, *others))[0]


def swap(value, axis, offset):
    size = lax.axis_size(axis)
    return lax.ppermute(value, axis, [(i, i ^ offset) for i in range(size)])


def spread(value, group):
    devices, parts = lax.axis_size("patch"), lax.axis_size("mp")
    pairs = [
        (device * parts + column, (device ^ (column + parts * group)) * parts + column)
        for device in range(devices)
        for column in range(parts)
    ]
    return lax.ppermute(value, ("patch", "mp"), pairs)


def swap_both(value, offset, column_offset):
    devices, parts = lax.axis_size("patch"), lax.axis_size("mp")
    pairs = [
        (device * parts + column, (device ^ offset) * parts + (column ^ column_offset))
        for device in range(devices)
        for column in range(parts)
    ]
    return lax.ppermute(value, ("patch", "mp"), pairs)


def each_device(count, body):
    group = min(count, UNROLL)
    if count == group:
        for step in range(count):
            body(step)
        return

    @pl.loop(0, count // group)
    def _(outer):
        for step in range(group):
            body(outer * group + step)


def term_kernel(
    cotangent_hbm, second_hbm, kept, sent, turned, cotangent, second, arrivals
):
    for copy in fetch([(cotangent_hbm, cotangent), (second_hbm, second)], arrivals):
        copy.wait()
    turned[...] = cotangent[...].T
    parts = lax.axis_size("mp")
    odd = lax.axis_index("mp") % 2 == 1
    term = lax.dot_general(
        second[...], cotangent[...], (((1,), (1,)), ((), ())), preferred_element_type=F32
    )
    size = term.shape[0] // parts
    for pair in range(parts // 2):
        even_block = term[2 * pair * size : (2 * pair + 1) * size]
        odd_block = term[(2 * pair + 1) * size : (2 * pair + 2) * size]
        kept[pair] = jnp.where(odd, odd_block, even_block)
        sent[pair] = jnp.where(odd, even_block, odd_block)


def pack_kernel(
    patches, cap, source_hbm, live_hbm, weight_hbm, payload, source, live, weight, arrivals
):
    own, column = lax.axis_index("patch"), lax.axis_index("mp")
    parts = lax.axis_size("mp")
    slots, rows, width = weight.shape
    copies = fetch([(source_hbm, source), (live_hbm, live), (weight_hbm, weight)], arrivals)
    tail = cap * rows
    row = lax.broadcasted_iota(jnp.int32, (INDEX_ROWS, width), 0)
    payload[...] = jnp.zeros_like(payload)
    for copy in copies:
        copy.wait()
    for slot in range(slots):
        device = source[slot] // patches
        place = source[slot] % patches
        rank = jnp.int32(0)
        for other in range(slot):
            same = (source[other] // patches == device) & (live[other] == 1)
            rank = rank + same.astype(jnp.int32)
        apart = device ^ own

        @pl.when((live[slot] == 1) & (apart % parts == column))
        def _():
            group = apart // parts
            payload[group, pl.ds(pl.multiple_of(rank * rows, rows), rows)] = weight[slot]
            old = payload[group, tail:].astype(F32)
            payload[group, tail:] = jnp.where(row == rank, place.astype(F32), old).astype(BF16)


def local_kernel(latent, first, second, hidden, message, slope, scratch):
    column = lax.axis_index("mp")
    rows = latent.shape[0]
    own = slope.shape[0]
    tile = min(256, rows)
    for start in range(0, rows, tile):
        here = pl.ds(start, tile)
        pre = dot(latent[here], first[...])
        scratch[...] = pre
        value = (pre * jax.nn.sigmoid(pre)).astype(BF16)
        hidden[here] = value
        message[here] = dot(value, second[...]).astype(BF16)
        mine = scratch[:, pl.ds(pl.multiple_of(column * own, own), own)]
        gate = jax.nn.sigmoid(mine)
        slope[:, here] = (gate * (1.0 + mine * (1.0 - gate))).T


def each_block(near, far, gather_order, body):
    own, column = lax.axis_index("patch"), lax.axis_index("mp")
    sides, groups = near.shape[:2]
    for turn in range(2 * sides):
        held = far if turn % 2 else near

        def one(group):
            apart = (column ^ turn) + 2 * sides * group
            position = jnp.int32(0)
            for place, offset in enumerate(gather_order):
                position = position + (((apart // offset) & 1) << place)
            number = turn * groups + group
            body(held.at[turn // 2, group], own ^ apart, position, number)

        each_device(groups, one)


def spot(apart, order):
    number = jnp.int32(0)
    for offset in order:
        number = 2 * number + ((apart // offset) & 1)
    return number


def halve(value, offset, sent, kept):
    half = value.shape[0] // 2
    upper = (lax.axis_index("patch") // offset) % 2 == 1
    kept[...] = jnp.where(upper, value[half:], value[:half])
    sent[:half] = jnp.where(upper, value[:half], value[half:]).astype(BF16)


def gradient_kernel(
    cap,
    gather_order,
    second_order,
    first_order,
    scaling,
    places,
    near,
    far,
    carried,
    message,
    hidden,
    slope_hbm,
    latent,
    sent_second,
    kept_second,
    forward,
    sent_first,
    kept_first,
    terms,
    forwards,
    total,
    slope,
    arrivals,
):
    copies = fetch([(slope_hbm, slope)], arrivals)
    own = lax.axis_index("patch")
    width = message.shape[1]
    rows = near.shape[3]
    patches = message.shape[0] // rows

    def one(held, device, position, number):
        turned = carried[position]
        summed = None
        for rank in range(cap):
            place = places[number * cap + rank]
            block = held[rank * rows : (rank + 1) * rows]
            start = pl.multiple_of(place * rows, rows)
            product = dot(block, message[pl.ds(start, rows)])
            summed = product if summed is None else summed + product
            terms[number * cap + rank] = dot(turned, block)
        forwards[spot(device ^ own, second_order)] = summed

    each_block(near, far, gather_order, one)
    total[...] = jnp.zeros_like(total)

    def add(slot):
        place = places[slot]
        term = terms[slot]
        total[place, :width] += term[:width].astype(BF16).astype(F32)
        total[place, width:] += term[width:]

    each_device(terms.shape[0], add)
    turned_message = jnp.concatenate(
        [total[place, :width].astype(BF16) for place in range(patches)], axis=1
    )
    second = dot(turned_message, hidden[...]) * scaling
    halve(second.T, second_order[0], sent_second, kept_second)
    for copy in copies:
        copy.wait()
    grad_pre = jnp.concatenate(
        [
            (total[place, width:] * slope[:, place * rows : (place + 1) * rows]).astype(BF16)
            for place in range(patches)
        ],
        axis=1,
    )
    first = dot(grad_pre, latent[...]) * scaling
    halve(first.T, first_order[0], sent_first, kept_first)
    devices = forwards.shape[0]
    split = kept_second.shape[0]
    for device in range(devices // 2):
        here = device * rows
        forward[here : here + rows] = forwards[device]
        sent_second[split + here : split + here + rows] = forwards[
            devices // 2 + device
        ].astype(BF16)


def finish_kernel(
    second_offset,
    first_offset,
    mesh_latent,
    forward,
    own_second,
    got_second,
    own_first,
    got_first,
    mesh_hbm,
    first_hbm,
    second_hbm,
    mesh,
    first,
    second,
    departures,
):
    mesh[...] = (mesh_latent[...].astype(F32) + forward[...]).astype(BF16)
    copies = []
    for place, offset, own, got, whole, target in (
        (0, second_offset, own_second, got_second, second, second_hbm),
        (1, first_offset, own_first, got_first, first, first_hbm),
    ):
        half = own.shape[0]
        upper = (lax.axis_index("patch") // offset) % 2
        whole[pl.ds(pl.multiple_of(upper * half, half), half)] = own[...].astype(F32)
        whole[pl.ds(pl.multiple_of((1 - upper) * half, half), half)] = got[...].astype(F32)
        copies.append(pltpu.make_async_copy(whole, target, departures.at[place]))
        copies[-1].start()
    copies.append(pltpu.make_async_copy(mesh, mesh_hbm, departures.at[2]))
    copies[-1].start()
    for copy in copies:
        copy.wait()


def per_device(
    grid_latent,
    mesh_latent,
    edge_weight,
    block_source,
    block_live,
    mlp_first,
    mlp_second,
    mesh_cotangent,
):
    devices = lax.axis_size("patch")
    parts = lax.axis_size("mp")
    slots, rows, _ = edge_weight.shape
    grid_rows, depth = grid_latent.shape
    patches = grid_rows // rows
    hidden_width, width = mlp_second.shape
    hidden_local = hidden_width // parts
    cap = -(-slots // devices)
    column = lax.axis_index("mp")
    scaling = 1.0 / math.sqrt(grid_rows * devices)
    payload_rows = cap * rows + INDEX_ROWS
    groups = devices // parts

    slot_bytes = ((slots,), jnp.int32)
    kept, sent, turned = call(
        term_kernel,
        "term",
        [(HBM, mesh_cotangent), (HBM, mlp_second)],
        [
            (VMEM, (parts // 2, hidden_local, rows), F32),
            (VMEM, (parts // 2, hidden_local, rows), F32),
            (VMEM, (width, rows), BF16),
        ],
        scratch=[
            VMEM(mesh_cotangent.shape, BF16),
            VMEM(mlp_second.shape, BF16),
            pltpu.SemaphoreType.DMA((2,)),
        ],
    )
    (payload,) = call(
        functools.partial(pack_kernel, patches, cap),
        "pack",
        [(HBM, block_source), (HBM, block_live), (HBM, edge_weight)],
        [(VMEM, (groups, payload_rows, rows), BF16)],
        scratch=[
            SMEM(*slot_bytes),
            SMEM(*slot_bytes),
            VMEM(edge_weight.shape, BF16),
            pltpu.SemaphoreType.DMA((3,)),
        ],
    )

    summed = after(kept, payload) + swap(sent, "mp", 1)
    offset = 2
    while summed.shape[0] > 2:
        pairs = summed.reshape(-1, 2, *summed.shape[1:])
        bit = (column // offset) % 2
        stay = lax.dynamic_index_in_dim(pairs, bit, 1, keepdims=False)
        away = lax.dynamic_index_in_dim(pairs, 1 - bit, 1, keepdims=False)
        summed = stay + swap(away, "mp", offset)
        offset *= 2
    bit = (column // offset) % 2
    stay = lax.dynamic_index_in_dim(summed, bit, 0, keepdims=False)
    away = lax.dynamic_index_in_dim(summed, 1 - bit, 0, keepdims=False).astype(BF16)
    steps = devices.bit_length() - 1
    up = [1 << place for place in range(steps)]
    down = up[::-1]
    gather_order, second_order, first_order = down[:1] + up[:-1], [*up[1::-1], *up[2:]], up
    across = gather_order[0]
    beside = swap(away, "mp", offset)
    facing = swap(jnp.concatenate([turned, stay.astype(BF16)]), "patch", across)
    corner = swap_both(away, across, offset)
    here = jnp.concatenate([turned, (stay + beside.astype(F32)).astype(BF16)])
    there = facing[width:].astype(F32) + corner.astype(F32)
    there = jnp.concatenate([facing[:width], there.astype(BF16)])
    carried = jnp.stack([here, there])

    latent = after(grid_latent, carried)
    hidden, message, slope = call(
        local_kernel,
        "local",
        [(VMEM, latent), (VMEM, mlp_first), (VMEM, mlp_second)],
        [
            (VMEM, (grid_rows, hidden_width), BF16),
            (VMEM, (grid_rows, width), BF16),
            (VMEM, (hidden_local, grid_rows), F32),
        ],
        scratch=[VMEM((min(256, grid_rows), hidden_width), F32)],
    )

    payload = after(payload, beside)
    spreads = [spread(payload[group], group) for group in range(groups)]
    for place in range(1, steps, 2):
        moves = gather_order[place : place + 2]
        offsets = [moves[0]] if len(moves) == 1 else [moves[0], moves[1], moves[0] ^ moves[1]]
        arriving = [swap(carried, "patch", offset) for offset in offsets]
        if place == 1:
            arriving[0] = after(arriving[0], hidden)
        carried = jnp.concatenate([carried, *arriving])

    blocks = jnp.stack(spreads)
    near = blocks[None]
    offset = parts // 2
    while offset > 1:
        near = jnp.concatenate([near, swap(near, "mp", offset)])
        offset //= 2
    far = swap(after(near, carried), "mp", 1)
    index_row = cap * rows
    places = jnp.stack([near, far], axis=1)[..., index_row : index_row + cap, 0]
    places = places.astype(jnp.int32).reshape(-1)

    sent_second, kept_second, forward, sent_first, kept_first = call(
        functools.partial(
            gradient_kernel, cap, gather_order, second_order, first_order, scaling
        ),
        "gradients",
        [
            (SMEM, places),
            (VMEM, near),
            (VMEM, far),
            (VMEM, carried),
            (VMEM, message),
            (VMEM, hidden),
            (HBM, slope),
            (VMEM, latent),
        ],
        [
            (VMEM, (hidden_width // 2 + devices // 2 * rows, width), BF16),
            (VMEM, (hidden_width // 2, width), F32),
            (VMEM, (devices // 2 * rows, width), F32),
            (VMEM, (depth // 2, hidden_local), BF16),
            (VMEM, (depth // 2, hidden_local), F32),
        ],
        scratch=[
            VMEM((devices * cap, width + hidden_local, rows), F32),
            VMEM((devices, rows, width), F32),
            VMEM((patches, width + hidden_local, rows), F32),
            VMEM(slope.shape, F32),
            pltpu.SemaphoreType.DMA((1,)),
        ],
    )

    split = hidden_width // 2
    for step in range(steps):
        got_second = swap(sent_second, "patch", second_order[step]).astype(F32)
        got_first = swap(sent_first, "patch", first_order[step]).astype(F32)
        second = kept_second + got_second[:split]
        forward = forward + got_second[split:]
        sent_first = (kept_first + got_first).astype(BF16)
        if step < steps - 1:
            size = forward.shape[0] // 2
            sent_second = jnp.concatenate([second, forward[size:]]).astype(BF16)
            forward = forward[:size]
            kept_second = sent_second[:split].astype(F32)
            kept_first = sent_first.astype(F32)
    second = second.astype(BF16)
    mesh_out, first, second = call(
        functools.partial(finish_kernel, second_order[0], first_order[0]),
        "finish",
        [
            (VMEM, mesh_latent),
            (VMEM, forward),
            (VMEM, second),
            (VMEM, swap(second, "patch", second_order[0])),
            (VMEM, sent_first),
            (VMEM, swap(sent_first, "patch", first_order[0])),
        ],
        [
            (HBM, (rows, width), BF16),
            (HBM, (depth, hidden_local), F32),
            (HBM, (hidden_width, width), F32),
        ],
        scratch=[
            VMEM((rows, width), BF16),
            VMEM((depth, hidden_local), F32),
            VMEM((hidden_width, width), F32),
            pltpu.SemaphoreType.DMA((3,)),
        ],
    )
    return (mesh_out, first, second)


def solution(mesh):
    placed = (
        P("patch", None),
        P("patch", "mp"),
        P("patch", None, None),
        P("patch"),
        P("patch"),
        P(),
        P(None, "mp"),
        P("patch", "mp"),
    )
    return jax.shard_map(
        per_device,
        mesh=mesh,
        in_specs=placed,
        out_specs=(P("patch", "mp"), P(None, "mp"), P(None, "mp")),
        check_vma=False,
    )
```

```python
import functools
import math

import jax
import jax.numpy as jnp
from jax import lax
from jax.experimental import pallas as pl
from jax.experimental.pallas import tpu as pltpu
from jax.sharding import PartitionSpec as P

BF16 = jnp.bfloat16
F32 = jnp.float32
INDEX_ROWS = 16
UNROLL = 8
VMEM_BYTES = 16 * 1024 * 1024
VMEM = pltpu.VMEM
SMEM = pltpu.SMEM
HBM = pltpu.HBM


def dot(left, right):
    return jnp.dot(left, right, preferred_element_type=F32)


def call(kernel, name, placed, outputs, scratch=(), cost=None):
    return pl.pallas_call(
        kernel,
        out_shape=[space(shape, dtype) for space, shape, dtype in outputs],
        in_specs=[pl.BlockSpec(memory_space=space) for space, _ in placed],
        out_specs=[pl.BlockSpec(memory_space=space) for space, _, _ in outputs],
        scratch_shapes=list(scratch),
        compiler_params=pltpu.CompilerParams(vmem_limit_bytes=VMEM_BYTES),
        cost_estimate=cost,
        name=name,
    )(
        *[
            operand if space is SMEM else pltpu.with_memory_space_constraint(operand, space)
            for space, operand in placed
        ]
    )


def fetch(pairs, arrivals):
    copies = [
        pltpu.make_async_copy(source, target, arrivals.at[place])
        for place, (source, target) in enumerate(pairs)
    ]
    for copy in copies:
        copy.start()
    return copies


def after(value, *others):
    return lax.optimization_barrier((value, *others))[0]


def swap(value, axis, offset):
    size = lax.axis_size(axis)
    return lax.ppermute(value, axis, [(i, i ^ offset) for i in range(size)])


def spread(value, group):
    devices, parts = lax.axis_size("patch"), lax.axis_size("mp")
    pairs = [
        (device * parts + column, (device ^ (column + parts * group)) * parts + column)
        for device in range(devices)
        for column in range(parts)
    ]
    return lax.ppermute(value, ("patch", "mp"), pairs)


def swap_both(value, offset, column_offset):
    devices, parts = lax.axis_size("patch"), lax.axis_size("mp")
    pairs = [
        (device * parts + column, (device ^ offset) * parts + (column ^ column_offset))
        for device in range(devices)
        for column in range(parts)
    ]
    return lax.ppermute(value, ("patch", "mp"), pairs)


def each_device(count, body):
    group = min(count, UNROLL)
    if count == group:
        for step in range(count):
            body(step)
        return

    @pl.loop(0, count // group)
    def _(outer):
        for step in range(group):
            body(outer * group + step)


def term_kernel(
    cotangent_hbm, second_hbm, kept, sent, turned, cotangent, second, arrivals
):
    for copy in fetch([(cotangent_hbm, cotangent), (second_hbm, second)], arrivals):
        copy.wait()
    turned[...] = cotangent[...].T
    parts = lax.axis_size("mp")
    odd = lax.axis_index("mp") % 2 == 1
    term = lax.dot_general(
        second[...], cotangent[...], (((1,), (1,)), ((), ())), preferred_element_type=F32
    )
    size = term.shape[0] // parts
    for pair in range(parts // 2):
        even_block = term[2 * pair * size : (2 * pair + 1) * size]
        odd_block = term[(2 * pair + 1) * size : (2 * pair + 2) * size]
        kept[pair] = jnp.where(odd, odd_block, even_block)
        sent[pair] = jnp.where(odd, even_block, odd_block)


def pack_kernel(
    patches, cap, source_hbm, live_hbm, weight_hbm, payload, source, live, weight, arrivals
):
    own, column = lax.axis_index("patch"), lax.axis_index("mp")
    parts = lax.axis_size("mp")
    slots, rows, width = weight.shape
    copies = fetch([(source_hbm, source), (live_hbm, live), (weight_hbm, weight)], arrivals)
    tail = cap * rows
    row = lax.broadcasted_iota(jnp.int32, (INDEX_ROWS, width), 0)
    payload[...] = jnp.zeros_like(payload)
    for copy in copies:
        copy.wait()
    for slot in range(slots):
        device = source[slot] // patches
        place = source[slot] % patches
        rank = jnp.int32(0)
        for other in range(slot):
            same = (source[other] // patches == device) & (live[other] == 1)
            rank = rank + same.astype(jnp.int32)
        apart = device ^ own

        @pl.when((live[slot] == 1) & (apart % parts == column))
        def _():
            group = apart // parts
            payload[group, pl.ds(pl.multiple_of(rank * rows, rows), rows)] = weight[slot]
            old = payload[group, tail:].astype(F32)
            payload[group, tail:] = jnp.where(row == rank, place.astype(F32), old).astype(BF16)


def local_kernel(latent, first, second, hidden, message, slope, scratch):
    column = lax.axis_index("mp")
    rows = latent.shape[0]
    own = slope.shape[0]
    tile = min(256, rows)
    for start in range(0, rows, tile):
        here = pl.ds(start, tile)
        pre = dot(latent[here], first[...])
        scratch[...] = pre
        value = (pre * jax.nn.sigmoid(pre)).astype(BF16)
        hidden[here] = value
        message[here] = dot(value, second[...]).astype(BF16)
        mine = scratch[:, pl.ds(pl.multiple_of(column * own, own), own)]
        gate = jax.nn.sigmoid(mine)
        slope[:, here] = (gate * (1.0 + mine * (1.0 - gate))).T


def each_block(near, far, gather_order, body):
    own, column = lax.axis_index("patch"), lax.axis_index("mp")
    sides, groups = near.shape[:2]
    for turn in range(2 * sides):
        held = far if turn % 2 else near

        def one(group):
            apart = (column ^ turn) + 2 * sides * group
            position = jnp.int32(0)
            for place, offset in enumerate(gather_order):
                position = position + (((apart // offset) & 1) << place)
            number = turn * groups + group
            body(held.at[turn // 2, group], own ^ apart, position, number)

        each_device(groups, one)


def spot(apart, order):
    number = jnp.int32(0)
    for offset in order:
        number = 2 * number + ((apart // offset) & 1)
    return number


def halve(value, offset, sent, kept):
    half = value.shape[0] // 2
    upper = (lax.axis_index("patch") // offset) % 2 == 1
    kept[...] = jnp.where(upper, value[half:], value[:half])
    sent[:half] = jnp.where(upper, value[:half], value[half:]).astype(BF16)


def gradient_kernel(
    cap,
    gather_order,
    second_order,
    first_order,
    scaling,
    places,
    near,
    far,
    carried,
    message,
    hidden,
    slope_hbm,
    latent,
    sent_second,
    kept_second,
    forward,
    sent_first,
    kept_first,
    terms,
    forwards,
    total,
    slope,
    arrivals,
):
    copies = fetch([(slope_hbm, slope)], arrivals)
    own = lax.axis_index("patch")
    width = message.shape[1]
    rows = near.shape[3]
    patches = message.shape[0] // rows

    def one(held, device, position, number):
        turned = carried[position]
        summed = None
        for rank in range(cap):
            place = places[number * cap + rank]
            block = held[rank * rows : (rank + 1) * rows]
            start = pl.multiple_of(place * rows, rows)
            product = dot(block, message[pl.ds(start, rows)])
            summed = product if summed is None else summed + product
            terms[number * cap + rank] = dot(turned, block)
        forwards[spot(device ^ own, second_order)] = summed

    each_block(near, far, gather_order, one)
    total[...] = jnp.zeros_like(total)

    def add(slot):
        place = places[slot]
        term = terms[slot]
        total[place, :width] += term[:width].astype(BF16).astype(F32)
        total[place, width:] += term[width:]

    each_device(terms.shape[0], add)
    turned_message = jnp.concatenate(
        [total[place, :width].astype(BF16) for place in range(patches)], axis=1
    )
    second = dot(turned_message, hidden[...]) * scaling
    halve(second.T, second_order[0], sent_second, kept_second)
    for copy in copies:
        copy.wait()
    grad_pre = jnp.concatenate(
        [
            (total[place, width:] * slope[:, place * rows : (place + 1) * rows]).astype(BF16)
            for place in range(patches)
        ],
        axis=1,
    )
    first = dot(grad_pre, latent[...]) * scaling
    halve(first.T, first_order[0], sent_first, kept_first)
    devices = forwards.shape[0]
    split = kept_second.shape[0]
    for device in range(devices // 2):
        here = device * rows
        forward[here : here + rows] = forwards[device]
        sent_second[split + here : split + here + rows] = forwards[
            devices // 2 + device
        ].astype(BF16)


def lay(offset, own, got, whole, target, departure):
    half = own.shape[0]
    upper = (lax.axis_index("patch") // offset) % 2
    whole[pl.ds(pl.multiple_of(upper * half, half), half)] = own[...].astype(F32)
    whole[pl.ds(pl.multiple_of((1 - upper) * half, half), half)] = got[...].astype(F32)
    copy = pltpu.make_async_copy(whole, target, departure)
    copy.start()
    return copy


def finish_first_kernel(
    offset, mesh_latent, forward, own, got, mesh_hbm, first_hbm, mesh, first, departures
):
    mesh[...] = (mesh_latent[...].astype(F32) + forward[...]).astype(BF16)
    out = pltpu.make_async_copy(mesh, mesh_hbm, departures.at[0])
    out.start()
    lay(offset, own, got, first, first_hbm, departures.at[1]).wait()
    out.wait()


def finish_second_kernel(offset, own, got, second_hbm, second, departures):
    lay(offset, own, got, second, second_hbm, departures.at[0]).wait()


def per_device(
    grid_latent,
    mesh_latent,
    edge_weight,
    block_source,
    block_live,
    mlp_first,
    mlp_second,
    mesh_cotangent,
):
    devices = lax.axis_size("patch")
    parts = lax.axis_size("mp")
    slots, rows, _ = edge_weight.shape
    grid_rows, depth = grid_latent.shape
    patches = grid_rows // rows
    hidden_width, width = mlp_second.shape
    hidden_local = hidden_width // parts
    cap = -(-slots // devices)
    column = lax.axis_index("mp")
    scaling = 1.0 / math.sqrt(grid_rows * devices)
    payload_rows = cap * rows + INDEX_ROWS
    groups = devices // parts

    slot_bytes = ((slots,), jnp.int32)
    kept, sent, turned = call(
        term_kernel,
        "term",
        [(HBM, mesh_cotangent), (HBM, mlp_second)],
        [
            (VMEM, (parts // 2, hidden_local, rows), F32),
            (VMEM, (parts // 2, hidden_local, rows), F32),
            (VMEM, (width, rows), BF16),
        ],
        scratch=[
            VMEM(mesh_cotangent.shape, BF16),
            VMEM(mlp_second.shape, BF16),
            pltpu.SemaphoreType.DMA((2,)),
        ],
    )
    (payload,) = call(
        functools.partial(pack_kernel, patches, cap),
        "pack",
        [(HBM, block_source), (HBM, block_live), (HBM, edge_weight)],
        [(VMEM, (groups, payload_rows, rows), BF16)],
        scratch=[
            SMEM(*slot_bytes),
            SMEM(*slot_bytes),
            VMEM(edge_weight.shape, BF16),
            pltpu.SemaphoreType.DMA((3,)),
        ],
    )

    summed = after(kept, payload) + swap(sent, "mp", 1)
    offset = 2
    while summed.shape[0] > 2:
        pairs = summed.reshape(-1, 2, *summed.shape[1:])
        bit = (column // offset) % 2
        stay = lax.dynamic_index_in_dim(pairs, bit, 1, keepdims=False)
        away = lax.dynamic_index_in_dim(pairs, 1 - bit, 1, keepdims=False)
        summed = stay + swap(away, "mp", offset)
        offset *= 2
    bit = (column // offset) % 2
    stay = lax.dynamic_index_in_dim(summed, bit, 0, keepdims=False)
    away = lax.dynamic_index_in_dim(summed, 1 - bit, 0, keepdims=False).astype(BF16)
    steps = devices.bit_length() - 1
    up = [1 << place for place in range(steps)]
    down = up[::-1]
    gather_order, second_order, first_order = down[:1] + up[:-1], [*up[1::-1], *up[2:]], up
    across = gather_order[0]
    beside = swap(away, "mp", offset)
    facing = swap(jnp.concatenate([turned, stay.astype(BF16)]), "patch", across)
    corner = swap_both(away, across, offset)
    here = jnp.concatenate([turned, (stay + beside.astype(F32)).astype(BF16)])
    there = facing[width:].astype(F32) + corner.astype(F32)
    there = jnp.concatenate([facing[:width], there.astype(BF16)])
    carried = jnp.stack([here, there])

    latent = after(grid_latent, carried)
    hidden, message, slope = call(
        local_kernel,
        "local",
        [(VMEM, latent), (VMEM, mlp_first), (VMEM, mlp_second)],
        [
            (VMEM, (grid_rows, hidden_width), BF16),
            (VMEM, (grid_rows, width), BF16),
            (VMEM, (hidden_local, grid_rows), F32),
        ],
        scratch=[VMEM((min(256, grid_rows), hidden_width), F32)],
    )

    payload = after(payload, beside)
    spreads = [spread(payload[group], group) for group in range(groups)]
    for place in range(1, steps, 2):
        moves = gather_order[place : place + 2]
        offsets = [moves[0]] if len(moves) == 1 else [moves[0], moves[1], moves[0] ^ moves[1]]
        arriving = [swap(carried, "patch", offset) for offset in offsets]
        if place == 1:
            arriving[0] = after(arriving[0], hidden)
        carried = jnp.concatenate([carried, *arriving])

    blocks = jnp.stack(spreads)
    near = blocks[None]
    offset = parts // 2
    while offset > 1:
        near = jnp.concatenate([near, swap(near, "mp", offset)])
        offset //= 2
    far = swap(after(near, carried), "mp", 1)
    index_row = cap * rows
    places = jnp.stack([near, far], axis=1)[..., index_row : index_row + cap, 0]
    places = places.astype(jnp.int32).reshape(-1)

    sent_second, kept_second, forward, sent_first, kept_first = call(
        functools.partial(
            gradient_kernel, cap, gather_order, second_order, first_order, scaling
        ),
        "gradients",
        [
            (SMEM, places),
            (VMEM, near),
            (VMEM, far),
            (VMEM, carried),
            (VMEM, message),
            (VMEM, hidden),
            (HBM, slope),
            (VMEM, latent),
        ],
        [
            (VMEM, (hidden_width // 2 + devices // 2 * rows, width), BF16),
            (VMEM, (hidden_width // 2, width), F32),
            (VMEM, (devices // 2 * rows, width), F32),
            (VMEM, (depth // 2, hidden_local), BF16),
            (VMEM, (depth // 2, hidden_local), F32),
        ],
        scratch=[
            VMEM((devices * cap, width + hidden_local, rows), F32),
            VMEM((devices, rows, width), F32),
            VMEM((patches, width + hidden_local, rows), F32),
            VMEM(slope.shape, F32),
            pltpu.SemaphoreType.DMA((1,)),
        ],
    )

    split = hidden_width // 2
    for step in range(steps):
        got_second = swap(sent_second, "patch", second_order[step]).astype(F32)
        got_first = swap(sent_first, "patch", first_order[step]).astype(F32)
        second = kept_second + got_second[:split]
        forward = forward + got_second[split:]
        sent_first = (kept_first + got_first).astype(BF16)
        if step < steps - 1:
            size = forward.shape[0] // 2
            sent_second = jnp.concatenate([second, forward[size:]]).astype(BF16)
            forward = forward[:size]
            kept_second = sent_second[:split].astype(F32)
            kept_first = sent_first.astype(F32)
    second = second.astype(BF16)
    mesh_out, first = call(
        functools.partial(finish_first_kernel, first_order[0]),
        "finish_first",
        [
            (VMEM, mesh_latent),
            (VMEM, forward),
            (VMEM, sent_first),
            (VMEM, swap(sent_first, "patch", first_order[0])),
        ],
        [(HBM, (rows, width), BF16), (HBM, (depth, hidden_local), F32)],
        scratch=[
            VMEM((rows, width), BF16),
            VMEM((depth, hidden_local), F32),
            pltpu.SemaphoreType.DMA((2,)),
        ],
    )
    (second,) = call(
        functools.partial(finish_second_kernel, second_order[0]),
        "finish_second",
        [(VMEM, second), (VMEM, swap(second, "patch", second_order[0]))],
        [(HBM, (hidden_width, width), F32)],
        scratch=[VMEM((hidden_width, width), F32), pltpu.SemaphoreType.DMA((1,))],
    )
    return (mesh_out, first, second)


def solution(mesh):
    placed = (
        P("patch", None),
        P("patch", "mp"),
        P("patch", None, None),
        P("patch"),
        P("patch"),
        P(),
        P(None, "mp"),
        P("patch", "mp"),
    )
    return jax.shard_map(
        per_device,
        mesh=mesh,
        in_specs=placed,
        out_specs=(P("patch", "mp"), P(None, "mp"), P(None, "mp")),
        check_vma=False,
    )
```
